256 devices in a mesh: emit: 32 (over y, z), panel: 8 (over x, core).
Axes of the slice: x: 4, y: 4, z: 8, core: 2. Of those that a mesh axis runs over, the one named last changes fastest.
Arguments:
- green_matrix: float32 [2, 196608, 1024], P(None, 'emit', 'panel'), may hold values from -120 to 120
- sign_bits: int32 [196608], P('emit'), may hold values from 0 to 1
- column_picks: int32 [1536], replicated, may hold values from 0 to 196607
Outputs:
- sketch: float32 [1536, 2, 1024], P('emit', None, 'panel')
The draws below stay inside these ranges and needn't reach their ends.
All inputs are finite; a program needn't handle non-finite values.
Results may differ from the reference program's by a relative error of at most 0.000094.
Values sent between devices are 32-bit elements; how exact they have to be, the bound alone decides.
A program may use at most 128 MiB of HBM per device.

```python
import math
import jax
import jax.numpy as jnp
from jax import lax

N1 = 384
N2 = 512
SKETCH = 1536
EMITTERS = 196608
RECEIVERS = 1024


def draw_green_matrix(key, part):
    key = jax.random.fold_in(key, 11)
    key_base = jax.random.fold_in(key, 1)
    key_rows = jax.random.fold_in(key, 2)
    key_cols = jax.random.fold_in(key, 3)
    entries = jax.random.truncated_normal(key_base, -4.0, 4.0, (2, EMITTERS, RECEIVERS), jnp.float32)
    ramp = 1.0 + 2.0 * jnp.arange(RECEIVERS, dtype=jnp.float32) / max(RECEIVERS - 1, 1)
    row_scale = ramp * jnp.exp(jax.random.uniform(key_rows, (RECEIVERS,), jnp.float32, 0.0, math.log(10.0)))
    col_scale = jnp.exp(jax.random.uniform(key_cols, (EMITTERS,), jnp.float32, 0.0, math.log(10.0)))
    scaled = entries * col_scale[None, :, None] * row_scale[None, None, :] * 0.25
    return jnp.clip(scaled, -120.0, 120.0)


def plant(values, stream_key, least, largest):
    spot = [jax.random.randint(jax.random.fold_in(stream_key, axis), (), 0, length) for axis, length in enumerate(values.shape)]
    main_axis = values.shape.index(max(values.shape))
    neighbour = spot[:main_axis] + [(spot[main_axis] + 1) % values.shape[main_axis]] + spot[main_axis + 1:]
    return values.at[tuple(spot)].set(least).at[tuple(neighbour)].set(largest)


def setup_inputs(seed: int = 0) -> dict:
    key_of = jax.random.split(jax.random.key(seed), 4)
    green_matrix = draw_green_matrix(jax.random.fold_in(key_of[3], 71), 0)
    sign_bits = plant(jax.random.randint(key_of[1], (EMITTERS,), 0, 2), jax.random.fold_in(key_of[1], 1), 0, 1).astype(jnp.int32)
    column_picks = plant(jax.random.randint(key_of[2], (SKETCH,), 0, EMITTERS), jax.random.fold_in(key_of[2], 1), 0, EMITTERS - 1).astype(jnp.int32)
    return {"green_matrix": green_matrix, "sign_bits": sign_bits, "column_picks": column_picks}


def phases(numerator, period):
    radians = -2.0 * math.pi / period * numerator.astype(jnp.float32)
    return (jnp.cos(radians), jnp.sin(radians))

def reference(green_matrix, sign_bits, column_picks):
    total_rows = green_matrix.shape[2]
    row_step = math.gcd(total_rows, 32)
    signs_float = (2 * sign_bits - 1).astype(jnp.float32)
    steps_b = jnp.arange(N2, dtype=jnp.int32)
    steps_a = jnp.arange(N1, dtype=jnp.int32)
    cos_b, sin_b = phases(steps_b[:, None] * steps_b[None, :] % N2, N2)
    twid_cos, twid_sin = phases(steps_b[:, None] * steps_a[None, :] % EMITTERS, EMITTERS)
    freq_high = column_picks // N2
    freq_part = column_picks % N2
    last_cos, last_sin = phases(freq_high[:, None] * steps_a[None, :] % N1, N1)
    highest = lax.Precision.HIGHEST

    def row_block(first_row):
        portion = lax.dynamic_slice_in_dim(green_matrix, first_row, row_step, 2)
        portion = portion * signs_float[None, :, None]
        portion = portion.reshape(2, N2, N1, row_step)
        real_in, imag_in = (portion[0], portion[1])
        real_mid = jnp.einsum('kb,bar->kar', cos_b, real_in, precision=highest) - jnp.einsum('kb,bar->kar', sin_b, imag_in, precision=highest)
        imag_mid = jnp.einsum('kb,bar->kar', sin_b, real_in, precision=highest) + jnp.einsum('kb,bar->kar', cos_b, imag_in, precision=highest)
        real_tw = real_mid * twid_cos[:, :, None] - imag_mid * twid_sin[:, :, None]
        imag_tw = real_mid * twid_sin[:, :, None] + imag_mid * twid_cos[:, :, None]
        real_pick = jnp.take(real_tw, freq_part, axis=0)
        imag_pick = jnp.take(imag_tw, freq_part, axis=0)
        real_out = lax.optimization_barrier(jnp.sum(real_pick * last_cos[:, :, None] - imag_pick * last_sin[:, :, None], axis=1))
        imag_out = lax.optimization_barrier(jnp.sum(real_pick * last_sin[:, :, None] + imag_pick * last_cos[:, :, None], axis=1))
        return jnp.stack([real_out, imag_out], axis=1)
    starts = jnp.arange(total_rows // row_step, dtype=jnp.int32) * row_step
    blocks = lax.map(row_block, starts)
    raw_sketch = jnp.moveaxis(blocks, 0, 2).reshape(SKETCH, 2, total_rows)
    norms = lax.optimization_barrier(jnp.sum(raw_sketch * raw_sketch, axis=(1, 2))) / total_rows
    return raw_sketch * lax.rsqrt(norms + 1e-06)[:, None, None]
```

```python
import functools
import math

import jax
import jax.numpy as jnp
from jax import lax
from jax.experimental import pallas as pl
from jax.experimental.pallas import tpu as pltpu
from jax.sharding import PartitionSpec as P

EMITTERS = 196608
SKETCH = 1536
LOCAL = 6144
INNER = 8
HALF = 384
DEPTH = 2 * HALF
LANES = 128
PICK_ROWS = SKETCH // LANES
SIGN_ROWS = LOCAL // LANES
CHUNK = 384


def wrap(values, period):
    return values - period * jnp.round(values * (1.0 / period))


def cos_sin(residue, period):
    t = residue * (math.pi / (2.0 * period))
    s = t * t
    sin = t * (1.0 + s * (-1.0 / 6 + s * (1.0 / 120 + s * (-1.0 / 5040 + s * (1.0 / 362880)))))
    versin = s * (0.5 + s * (-1.0 / 24 + s * (1.0 / 720 + s * (-1.0 / 40320))))
    cos = 1.0 - versin
    sin, cos = 2.0 * sin * cos, 1.0 - 2.0 * sin * sin
    return 1.0 - 2.0 * sin * sin, 2.0 * sin * cos


def split(values):
    high = values.astype(jnp.bfloat16)
    return high, (values - high.astype(jnp.float32)).astype(jnp.bfloat16)


def local_kernel(x_hbm, sign_ref, pick_ref, out_ref, x, fold, rhs, lhs_h, lhs_l, kb, w, pre, pad, tr, acc, sems):
    position = lax.axis_index("emit")
    parts = 8
    rows = LOCAL // parts
    copies = []
    for part in range(parts):
        sl = pl.ds(part * rows, rows)
        copy = pltpu.make_async_copy(x_hbm.at[:, sl], x.at[:, sl], sems.at[part])
        copy.start()
        copies.append(copy)

    pad[...] = jnp.zeros_like(pad)
    k = pick_ref[...]
    kf = k.astype(jnp.float32)
    turn = 6144 * ((position * k) & 31) + 3068 * k
    turn = turn - EMITTERS * jnp.round(turn.astype(jnp.float32) * (1.0 / EMITTERS)).astype(jnp.int32)
    reduced = wrap(kf, 49152.0)
    w_cos, w_sin = cos_sin(wrap(kf, float(EMITTERS)), float(EMITTERS))
    p_cos, p_sin = cos_sin(turn.astype(jnp.float32), float(EMITTERS))
    r_cos, r_sin = cos_sin(wrap(reduced * 256.0, 49152.0), 49152.0)
    for slot, value in enumerate((reduced, w_cos, w_sin, p_cos, p_sin, r_cos, r_sin)):
        pad[slot * 16 : slot * 16 + PICK_ROWS] = value
    tr[0] = pad[...].T
    pad[0:SIGN_ROWS] = (2 * sign_ref[...] - 1).astype(jnp.float32)
    tr[1] = pad[...].T
    for q in range(PICK_ROWS):
        sl = slice(q * LANES, (q + 1) * LANES)

        def column(slot):
            c = slot * 16 + q
            return jnp.broadcast_to(tr[0, :, c : c + 1], (LANES, LANES))

        kb[0, sl] = column(0)
        w[0, sl] = column(1)
        w[1, sl] = column(2)
        pre[0, sl] = column(3)
        pre[1, sl] = column(4)
        kb[1, sl] = column(5)
        kb[2, sl] = column(6)

    odd = (2 * lax.broadcasted_iota(jnp.int32, (16, LANES), 1) + 1).astype(jnp.float32)

    @pl.loop(0, SKETCH // 16, unroll=2)
    def _(t):
        sl = pl.ds(pl.multiple_of(t * 16, 16), 16)
        cos, sin = cos_sin(wrap(kb[0, sl] * odd, 49152.0), 49152.0)
        r_cos = kb[1, sl]
        r_sin = kb[2, sl]
        for g in range(3):
            for base, value in ((0, cos), (HALF, sin)):
                high, low = split(value)
                lanes = slice(base + g * LANES, base + (g + 1) * LANES)
                lhs_h[sl, lanes] = high
                lhs_l[sl, lanes] = low
            if g < 2:
                cos, sin = cos * r_cos - sin * r_sin, sin * r_cos + cos * r_sin

    for copy in copies:
        copy.wait()

    for upper in range(SIGN_ROWS // 2, SIGN_ROWS):
        lower = SIGN_ROWS - 1 - upper
        sign_u = jnp.broadcast_to(tr[1, :, upper : upper + 1], (LANES, LANES))
        sign_l = jnp.broadcast_to(tr[1, :, lower : lower + 1], (LANES, LANES))
        for part in range(2):
            above = x[part, upper * LANES : (upper + 1) * LANES] * sign_u
            below = x[part, lower * LANES : (lower + 1) * LANES] * sign_l
            below = jnp.concatenate([below[8 * t : 8 * t + 8] for t in range(15, -1, -1)], axis=0)
            sl = slice((upper - SIGN_ROWS // 2) * LANES, (upper - SIGN_ROWS // 2 + 1) * LANES)
            fold[part, 0, sl] = above + below
            fold[part, 1, sl] = above - below

    @pl.loop(0, INNER)
    def _(i):
        pick = pl.ds(i, HALF, stride=INNER)
        quarters = (
            (fold[0, 0, pick], 0, 0),
            (fold[1, 0, pick], 0, LANES),
            (fold[1, 1, pick], HALF, 0),
            (-fold[0, 1, pick], HALF, LANES),
        )
        for value, row, lane in quarters:
            high, low = split(value)
            lanes = slice(lane, lane + LANES)
            rhs[i, row : row + HALF, lanes] = high
            rhs[i, DEPTH + row : DEPTH + row + HALF, lanes] = low
            rhs[i, 2 * DEPTH + row : 2 * DEPTH + row + HALF, lanes] = high

    @pl.loop(0, SKETCH // CHUNK)
    def _(c):
        sl = pl.ds(pl.multiple_of(c * CHUNK, CHUNK), CHUNK)
        acc[...] = jnp.zeros_like(acc)

        @pl.loop(0, INNER)
        def _(step):
            high = lhs_h[sl]
            lhs = jnp.concatenate([high, high, lhs_l[sl]], axis=1)
            y = jnp.dot(lhs, rhs[INNER - 1 - step], preferred_element_type=jnp.float32)
            real, imag = acc[:, :LANES], acc[:, LANES:]
            cos, sin = w[0, sl], w[1, sl]
            acc[:, :LANES] = real * cos + imag * sin + y[:, :LANES]
            acc[:, LANES:] = imag * cos - real * sin + y[:, LANES:]

        real, imag = acc[:, :LANES], acc[:, LANES:]
        cos, sin = pre[0, sl], pre[1, sl]
        out_ref[sl, :LANES] = real * cos + imag * sin
        out_ref[sl, LANES:] = imag * cos - real * sin


def local_sketch(green_matrix, sign_bits, column_picks):
    f32, bf16 = jnp.float32, jnp.bfloat16
    return pl.pallas_call(
        local_kernel,
        out_shape=jax.ShapeDtypeStruct((SKETCH, 2 * LANES), f32),
        in_specs=[
            pl.BlockSpec(memory_space=pl.ANY),
            pl.BlockSpec(memory_space=pltpu.VMEM),
            pl.BlockSpec(memory_space=pltpu.VMEM),
        ],
        out_specs=pl.BlockSpec(memory_space=pltpu.VMEM),
        scratch_shapes=[
            pltpu.VMEM((2, LOCAL, LANES), f32),
            pltpu.VMEM((2, 2, LOCAL // 2, LANES), f32),
            pltpu.VMEM((INNER, 3 * DEPTH, 2 * LANES), bf16),
            pltpu.VMEM((SKETCH, DEPTH), bf16),
            pltpu.VMEM((SKETCH, DEPTH), bf16),
            pltpu.VMEM((3, SKETCH, LANES), f32),
            pltpu.VMEM((2, SKETCH, LANES), f32),
            pltpu.VMEM((2, SKETCH, LANES), f32),
            pltpu.VMEM((LANES, LANES), f32),
            pltpu.VMEM((2, LANES, LANES), f32),
            pltpu.VMEM((CHUNK, 2 * LANES), f32),
            pltpu.SemaphoreType.DMA((8,)),
        ],
        compiler_params=pltpu.CompilerParams(vmem_limit_bytes=56 * 1024 * 1024),
    )(green_matrix, sign_bits.reshape(SIGN_ROWS, LANES), column_picks.reshape(PICK_ROWS, LANES))


def body(green_matrix, sign_bits, column_picks):
    partial = local_sketch(green_matrix, sign_bits, column_picks)
    raw_sketch = lax.psum_scatter(partial, "emit", scatter_dimension=0, tiled=True)
    energy = jnp.sum(raw_sketch * raw_sketch, axis=1)
    column_total = lax.psum(energy, "panel")
    inverse_norm = lax.rsqrt(column_total / (LANES * lax.axis_size("panel")) + 1e-06)
    return (raw_sketch * inverse_norm[:, None]).reshape(-1, 2, LANES)


def solution(mesh):
    placed = (P(None, "emit", "panel"), P("emit"), P())
    return jax.shard_map(
        body, mesh=mesh, in_specs=placed, out_specs=P("emit", None, "panel"), check_vma=False
    )
```

```python
import math

import jax
import jax.numpy as jnp
from jax import lax
from jax.experimental import pallas as pl
from jax.experimental.pallas import tpu as pltpu
from jax.sharding import PartitionSpec as P

EMITTERS = 196608
SKETCH = 1536
LOCAL = 6144
INNER = 8
HALF = 384
DEPTH = 2 * HALF
LANES = 128
PICK_ROWS = SKETCH // LANES
SIGN_ROWS = LOCAL // LANES
RING_Z = 8
RING_Y = 4
PANELS = 8
OWN = SKETCH // (RING_Z * RING_Y)
BLOCK = OWN * RING_Y


MESH = pl.DeviceIdType.MESH


def wrap(values, period):
    return values - period * jnp.round(values * (1.0 / period))


def cos_sin(residue, period):
    t = residue * (math.pi / (2.0 * period))
    s = t * t
    sin = t * (1.0 + s * (-1.0 / 6 + s * (1.0 / 120 + s * (-1.0 / 5040 + s * (1.0 / 362880)))))
    versin = s * (0.5 + s * (-1.0 / 24 + s * (1.0 / 720 + s * (-1.0 / 40320))))
    cos = 1.0 - versin
    sin, cos = 2.0 * sin * cos, 1.0 - 2.0 * sin * sin
    return 1.0 - 2.0 * sin * sin, 2.0 * sin * cos


def split(values):
    high = values.astype(jnp.bfloat16)
    return high, (values - high.astype(jnp.float32)).astype(jnp.bfloat16)


def kernel(
    x_hbm, sign_ref, pick_ref, out_ref,
    x, fold, rhs_h, rhs_l, lhs_h, lhs_l, kb, w, pre, pad, tr, acc,
    z_out, z_in, y_in, energy, n_in,
    x_sem, z_send, z_recv, y_send, y_recv, n_send, n_recv,
):
    position = lax.axis_index("emit")
    panel = lax.axis_index("panel")
    y_here, z_here = position // RING_Z, position % RING_Z

    def at_z(d):
        return {"emit": y_here * RING_Z + (z_here + d) % RING_Z}

    def at_y(d):
        return {"emit": (y_here + d) % RING_Y * RING_Z + z_here}

    def at_panel(d):
        return {"panel": (panel + d) % PANELS}

    parts = 8
    rows = LOCAL // parts
    copies = []
    for part in range(parts):
        sl = pl.ds(part * rows, rows)
        copy = pltpu.make_async_copy(x_hbm.at[:, sl], x.at[:, sl], x_sem.at[part])
        copy.start()
        copies.append(copy)

    barrier = pltpu.get_barrier_semaphore()
    partners = [at_z(1), at_z(-1)]
    partners += [at_y(d) for d in range(1, RING_Y)]
    partners += [at_panel(d) for d in range(1, PANELS)]
    for partner in partners:
        pl.semaphore_signal(barrier, inc=1, device_id=partner, device_id_type=MESH)

    pad[...] = jnp.zeros_like(pad)
    k = pick_ref[...]
    kf = k.astype(jnp.float32)
    turn = 6144 * ((position * k) & 31) + 3068 * k
    turn = turn - EMITTERS * jnp.round(turn.astype(jnp.float32) * (1.0 / EMITTERS)).astype(jnp.int32)
    reduced = wrap(kf, 49152.0)
    w_cos, w_sin = cos_sin(wrap(kf, float(EMITTERS)), float(EMITTERS))
    p_cos, p_sin = cos_sin(turn.astype(jnp.float32), float(EMITTERS))
    r_cos, r_sin = cos_sin(wrap(reduced * 256.0, 49152.0), 49152.0)
    for slot, value in enumerate((reduced, w_cos, w_sin, p_cos, p_sin, r_cos, r_sin)):
        pad[slot * 16 : slot * 16 + PICK_ROWS] = value
    tr[0] = pad[...].T
    pad[0:SIGN_ROWS] = (2 * sign_ref[...] - 1).astype(jnp.float32)
    tr[1] = pad[...].T
    for q in range(PICK_ROWS):
        sl = slice(q * LANES, (q + 1) * LANES)
        for slot, ref in enumerate(
            (kb.at[0], w.at[0], w.at[1], pre.at[0], pre.at[1], kb.at[1], kb.at[2])
        ):
            c = slot * 16 + q
            ref[sl] = jnp.broadcast_to(tr[0, :, c : c + 1], (LANES, LANES))

    odd = (2 * lax.broadcasted_iota(jnp.int32, (16, LANES), 1) + 1).astype(jnp.float32)

    @pl.loop(0, SKETCH // 16)
    def _(t):
        sl = pl.ds(pl.multiple_of(t * 16, 16), 16)
        cos, sin = cos_sin(wrap(kb[0, sl] * odd, 49152.0), 49152.0)
        r_cos, r_sin = kb[1, sl], kb[2, sl]
        for g in range(3):
            if g:
                cos, sin = cos * r_cos - sin * r_sin, sin * r_cos + cos * r_sin
            for base, value in ((0, cos), (HALF, sin)):
                high, low = split(value)
                lanes = slice(base + g * LANES, base + (g + 1) * LANES)
                lhs_h[sl, lanes] = high
                lhs_l[sl, lanes] = low

    for copy in copies:
        copy.wait()

    for upper in range(SIGN_ROWS // 2, SIGN_ROWS):
        lower = SIGN_ROWS - 1 - upper
        sign_u = jnp.broadcast_to(tr[1, :, upper : upper + 1], (LANES, LANES))
        sign_l = jnp.broadcast_to(tr[1, :, lower : lower + 1], (LANES, LANES))
        sl = slice((upper - SIGN_ROWS // 2) * LANES, (upper - SIGN_ROWS // 2 + 1) * LANES)
        for part in range(2):
            above = x[part, upper * LANES : (upper + 1) * LANES] * sign_u
            below = x[part, lower * LANES : (lower + 1) * LANES] * sign_l
            below = jnp.concatenate([below[8 * t : 8 * t + 8] for t in range(15, -1, -1)], axis=0)
            fold[part, 0, sl] = above + below
            fold[part, 1, sl] = above - below

    @pl.loop(0, INNER)
    def _(i):
        pick = pl.ds(i, HALF, stride=INNER)
        quarters = (
            (fold[0, 0, pick], 0, 0),
            (fold[1, 0, pick], 0, LANES),
            (fold[1, 1, pick], HALF, 0),
            (-fold[0, 1, pick], HALF, LANES),
        )
        for value, row, lane in quarters:
            high, low = split(value)
            lanes = slice(lane, lane + LANES)
            rhs_h[i, row : row + HALF, lanes] = high
            rhs_l[i, row : row + HALF, lanes] = low

    def group(targets):
        slices = []
        for d, _ in targets:
            block = (z_here + d) % RING_Z
            slices.append(pl.ds(pl.multiple_of(block * BLOCK, BLOCK), BLOCK))
        for step in range(INNER):
            i = INNER - 1 - step
            high = jnp.concatenate([lhs_h[sl] for sl in slices], axis=0)
            low = jnp.concatenate([lhs_l[sl] for sl in slices], axis=0)
            lhs = jnp.concatenate([high, high, low], axis=1)
            xh = rhs_h[i]
            both = jnp.concatenate([xh, rhs_l[i], xh], axis=0)
            product = jnp.dot(lhs, both, preferred_element_type=jnp.float32)
            for n, sl in enumerate(slices):
                mine = slice(n * BLOCK, (n + 1) * BLOCK)
                new_real, new_imag = product[mine, :LANES], product[mine, LANES:]
                if step:
                    real, imag = acc[mine, :LANES], acc[mine, LANES:]
                    cos, sin = w[0, sl], w[1, sl]
                    new_real = real * cos + imag * sin + new_real
                    new_imag = imag * cos - real * sin + new_imag
                if i:
                    acc[mine, :LANES] = new_real
                    acc[mine, LANES:] = new_imag
                else:
                    cos, sin = pre[0, sl], pre[1, sl]
                    ref = targets[n][1]
                    ref[:, :LANES] = new_real * cos + new_imag * sin
                    ref[:, LANES:] = new_imag * cos - new_real * sin

    def z_copy(way, step, part=slice(None)):
        return pltpu.make_async_remote_copy(
            src_ref=z_out.at[way, step, part],
            dst_ref=z_in.at[way, step, part],
            send_sem=z_send.at[way, step],
            recv_sem=z_recv.at[way, step],
            device_id=at_z(1 - 2 * way),
            device_id_type=MESH,
        )

    half = BLOCK // 2
    halves = (pl.ds(0, half), pl.ds(half, half))
    group([(4, z_out.at[0, 0])])
    z_out[1, 0, half:] = z_out[0, 0, half:]
    pl.semaphore_wait(barrier, len(partners))
    sent = [z_copy(way, 0, halves[way]) for way in range(2)]
    for copy in sent:
        copy.start()
    last = sent
    for step in range(1, 4):
        group([(4 - step, z_out.at[0, step]), (step - 4, z_out.at[1, step])])
        copies = []
        for way in range(2):
            last[way].wait_recv()
            part = halves[way] if step == 1 else slice(None)
            z_out[way, step, part] += z_in[way, step - 1, part]
            copies.append(z_copy(way, step))
            copies[way].start()
        last = copies
        sent = sent + copies
    group([(0, acc.at[:BLOCK])])
    for way in range(2):
        last[way].wait_recv()
        acc[:BLOCK] += z_in[way, 3]

    copies = []
    for d in range(1, RING_Y):
        block = (y_here + d) % RING_Y
        copy = pltpu.make_async_remote_copy(
            src_ref=acc.at[pl.ds(pl.multiple_of(block * OWN, OWN), OWN)],
            dst_ref=y_in.at[d - 1],
            send_sem=y_send.at[d - 1],
            recv_sem=y_recv.at[d - 1],
            device_id=at_y(d),
            device_id_type=MESH,
        )
        copy.start()
        copies.append(copy)
    sent = sent + copies
    raw = acc[pl.ds(pl.multiple_of(y_here * OWN, OWN), OWN)]
    for d, copy in enumerate(copies):
        copy.wait_recv()
        raw = raw + y_in[d]

    real, imag = raw[:, :LANES], raw[:, LANES:]
    pad[...] = jnp.zeros_like(pad)
    pad[:OWN] = real * real + imag * imag
    total = jnp.sum(pad[...].T, axis=0, keepdims=True)
    energy[...] = jnp.broadcast_to(total, energy.shape)
    copies = []
    for d in range(1, PANELS):
        copy = pltpu.make_async_remote_copy(
            src_ref=energy,
            dst_ref=n_in.at[d - 1],
            send_sem=n_send.at[d - 1],
            recv_sem=n_recv.at[d - 1],
            device_id=at_panel(d),
            device_id_type=MESH,
        )
        copy.start()
        copies.append(copy)
    sent = sent + copies
    for d, copy in enumerate(copies):
        copy.wait_recv()
        total = total + n_in[d, :1]
    scale = lax.rsqrt(total * (1.0 / (LANES * PANELS)) + 1e-06)
    scale = jnp.broadcast_to(scale, (LANES, LANES)).T[:OWN]
    out_ref[:, :LANES] = real * scale
    out_ref[:, LANES:] = imag * scale
    for copy in sent:
        copy.wait_send()


def fused(green_matrix, sign_bits, picks):
    f32, bf16 = jnp.float32, jnp.bfloat16
    wide = 2 * LANES
    return pl.pallas_call(
        kernel,
        out_shape=jax.ShapeDtypeStruct((OWN, wide), f32),
        in_specs=[
            pl.BlockSpec(memory_space=pl.ANY),
            pl.BlockSpec(memory_space=pltpu.VMEM),
            pl.BlockSpec(memory_space=pltpu.VMEM),
        ],
        out_specs=pl.BlockSpec(memory_space=pltpu.VMEM),
        scratch_shapes=[
            pltpu.VMEM((2, LOCAL, LANES), f32),
            pltpu.VMEM((2, 2, LOCAL // 2, LANES), f32),
            pltpu.VMEM((INNER, DEPTH, wide), bf16),
            pltpu.VMEM((INNER, DEPTH, wide), bf16),
            pltpu.VMEM((SKETCH, DEPTH), bf16),
            pltpu.VMEM((SKETCH, DEPTH), bf16),
            pltpu.VMEM((3, SKETCH, LANES), f32),
            pltpu.VMEM((2, SKETCH, LANES), f32),
            pltpu.VMEM((2, SKETCH, LANES), f32),
            pltpu.VMEM((LANES, LANES), f32),
            pltpu.VMEM((2, LANES, LANES), f32),
            pltpu.VMEM((2 * BLOCK, wide), f32),
            pltpu.VMEM((2, 4, BLOCK, wide), f32),
            pltpu.VMEM((2, 4, BLOCK, wide), f32),
            pltpu.VMEM((RING_Y - 1, OWN, wide), f32),
            pltpu.VMEM((8, LANES), f32),
            pltpu.VMEM((PANELS - 1, 8, LANES), f32),
            pltpu.SemaphoreType.DMA((8,)),
            pltpu.SemaphoreType.DMA((2, 4)),
            pltpu.SemaphoreType.DMA((2, 4)),
            pltpu.SemaphoreType.DMA((RING_Y - 1,)),
            pltpu.SemaphoreType.DMA((RING_Y - 1,)),
            pltpu.SemaphoreType.DMA((PANELS - 1,)),
            pltpu.SemaphoreType.DMA((PANELS - 1,)),
        ],
        compiler_params=pltpu.CompilerParams(
            collective_id=0, has_side_effects=True, vmem_limit_bytes=56 * 1024 * 1024
        ),
    )(green_matrix, sign_bits, picks)


def body(green_matrix, sign_bits, column_picks):
    picks = column_picks.reshape(RING_Y, RING_Z, OWN).transpose(1, 0, 2).reshape(PICK_ROWS, LANES)
    sketch = fused(green_matrix, sign_bits.reshape(SIGN_ROWS, LANES), picks)
    return sketch.reshape(OWN, 2, LANES)


def solution(mesh):
    placed = (P(None, "emit", "panel"), P("emit"), P())
    return jax.shard_map(
        body, mesh=mesh, in_specs=placed, out_specs=P("emit", None, "panel"), check_vma=False
    )
```

```python
import math

import jax
import jax.numpy as jnp
from jax import lax
from jax.experimental import pallas as pl
from jax.experimental.pallas import tpu as pltpu
from jax.sharding import PartitionSpec as P

EMITTERS = 196608
SKETCH = 1536
LOCAL = 6144
INNER = 8
HALF = 384
DEPTH = 2 * HALF
LANES = 128
PICK_ROWS = SKETCH // LANES
SIGN_ROWS = LOCAL // LANES
RING_Z = 8
RING_Y = 4
PANELS = 8
OWN = SKETCH // (RING_Z * RING_Y)
PART = OWN // 2
BLOCK_A = PART * RING_Y
BLOCK_B = PART * RING_Z
START_B = BLOCK_A * RING_Z
TILE = 32
FINE = jnp.float8_e4m3fn
STEP = 512.0
GROUPS = (
    (("a", 3), ("a", -3), ("b", 2)),
    (("a", 4), ("b", 1)),
    (("a", 1), ("a", -1), ("b", -1)),
    (("a", 2), ("a", -2)),
    (("b", 0), ("a", 0)),
)


MESH = pl.DeviceIdType.MESH


def wrap(values, period):
    return values - period * jnp.round(values * (1.0 / period))


def cos_sin(residue, period):
    t = residue * (math.pi / (2.0 * period))
    s = t * t
    sin = t * (1.0 + s * (-1.0 / 6 + s * (1.0 / 120 + s * (-1.0 / 5040 + s * (1.0 / 362880)))))
    versin = s * (0.5 + s * (-1.0 / 24 + s * (1.0 / 720 + s * (-1.0 / 40320))))
    cos = 1.0 - versin
    sin, cos = 2.0 * sin * cos, 1.0 - 2.0 * sin * sin
    return 1.0 - 2.0 * sin * sin, 2.0 * sin * cos


def table_row(column):
    owner, rest = divmod(column, OWN)
    y, z = divmod(owner, RING_Z)
    if rest < PART:
        return z * BLOCK_A + y * PART + rest
    return START_B + y * BLOCK_B + z * PART + rest - PART


def size(half):
    return BLOCK_A if half == "a" else BLOCK_B


def rows_before(group):
    return sum(size(half) for blocks in GROUPS[:group] for half, _ in blocks)


def kernel(
    x_hbm, sign_ref, pick_ref, out_ref,
    x, fold, rhs_h, rhs_l, lhs_h, lhs_l, kb, w, pre, pad, tr, acc, sum_a, sum_b,
    a_out, a_in, ya_in, b_out, b_in, zb_in, energy, n_in,
    x_sem, a_send, a_recv, ya_send, ya_recv, b_send, b_recv, zb_send, zb_recv, n_send, n_recv,
):
    position = lax.axis_index("emit")
    panel = lax.axis_index("panel")
    y_here, z_here = position // RING_Z, position % RING_Z

    def at_z(d):
        return {"emit": y_here * RING_Z + (z_here + d) % RING_Z}

    def at_y(d):
        return {"emit": (y_here + d) % RING_Y * RING_Z + z_here}

    def at_panel(d):
        return {"panel": (panel + d) % PANELS}

    parts = 8
    rows = LOCAL // parts
    copies = {}
    for part in (3, 4, 2, 5, 1, 6, 0, 7):
        sl = pl.ds(part * rows, rows)
        copies[part] = pltpu.make_async_copy(x_hbm.at[:, sl], x.at[:, sl], x_sem.at[part])
        copies[part].start()

    barrier = pltpu.get_barrier_semaphore()
    partners = [at_z(d) for d in range(1, RING_Z)]
    partners += [at_y(d) for d in range(1, RING_Y)]
    partners += [at_panel(d) for d in range(1, PANELS)]
    for partner in partners:
        pl.semaphore_signal(barrier, inc=1, device_id=partner, device_id_type=MESH)

    pad[...] = jnp.zeros_like(pad)
    k = pick_ref[...].reshape(PICK_ROWS, LANES)
    kf = k.astype(jnp.float32)
    turn = 6144 * ((position * k) & 31) + 3068 * k
    turn = turn - EMITTERS * jnp.round(turn.astype(jnp.float32) * (1.0 / EMITTERS)).astype(jnp.int32)
    reduced = wrap(kf, 49152.0)
    w_cos, w_sin = cos_sin(wrap(kf, float(EMITTERS)), float(EMITTERS))
    p_cos, p_sin = cos_sin(turn.astype(jnp.float32), float(EMITTERS))
    r_cos, r_sin = cos_sin(wrap(reduced * 256.0, 49152.0), 49152.0)
    for slot, value in enumerate((reduced, w_cos, w_sin, p_cos, p_sin, r_cos, r_sin)):
        pad[slot * 16 : slot * 16 + PICK_ROWS] = value
    tr[0] = pad[...].T
    pad[0:SIGN_ROWS] = (2 * sign_ref[...].reshape(SIGN_ROWS, LANES) - 1).astype(jnp.float32)
    tr[1] = pad[...].T
    for q in range(PICK_ROWS):
        for slot, ref in enumerate(
            (kb.at[0], w.at[0], w.at[1], pre.at[0], pre.at[1], kb.at[1], kb.at[2])
        ):
            c = slot * 16 + q
            spread = jnp.broadcast_to(tr[0, :, c : c + 1], (LANES, LANES))
            for first in range(0, LANES, 8):
                row = table_row(q * LANES + first)
                ref[row : row + 8] = spread[first : first + 8]

    odd = (2 * lax.broadcasted_iota(jnp.int32, (TILE, LANES), 1) + 1).astype(jnp.float32)

    def source(half, d):
        if half == "a":
            return pl.multiple_of((z_here + d) % RING_Z * BLOCK_A, TILE)
        return pl.multiple_of(START_B + (y_here + d) % RING_Y * BLOCK_B, TILE)

    def table_tile(first, row):
        sl = pl.ds(first, TILE)
        to = pl.ds(row, TILE)
        cos, sin = cos_sin(wrap(kb[0, sl] * odd, 49152.0), 49152.0)
        r_cos, r_sin = kb[1, sl], kb[2, sl]
        for g in range(3):
            if g:
                cos, sin = cos * r_cos - sin * r_sin, sin * r_cos + cos * r_sin
            for base, value in ((0, cos), (HALF, sin)):
                high = value.astype(jnp.bfloat16)
                lane = base + g * LANES
                lhs_h[to, lane : lane + LANES] = high
                lhs_l[to, lane : lane + LANES] = value.astype(FINE)
                rest = (value - high.astype(jnp.float32)) * STEP
                lhs_l[to, DEPTH + lane : DEPTH + lane + LANES] = rest.astype(FINE)

    row = 0
    for half, d in GROUPS[0]:
        first = source(half, d)

        @pl.loop(0, size(half) // TILE)
        def _(t, first=first, row=row):
            table_tile(
                pl.multiple_of(first + t * TILE, TILE), pl.multiple_of(row + t * TILE, TILE)
            )

        row += size(half)

    peak = jnp.zeros((LANES, LANES), jnp.float32)
    for upper in range(SIGN_ROWS // 2, SIGN_ROWS):
        lower = SIGN_ROWS - 1 - upper
        if upper * LANES % rows == 0:
            copies[upper * LANES // rows].wait()
            copies[lower * LANES // rows].wait()
        sign_u = jnp.broadcast_to(tr[1, :, upper : upper + 1], (LANES, LANES))
        sign_l = jnp.broadcast_to(tr[1, :, lower : lower + 1], (LANES, LANES))
        sl = slice((upper - SIGN_ROWS // 2) * LANES, (upper - SIGN_ROWS // 2 + 1) * LANES)
        for part in range(2):
            above = x[part, upper * LANES : (upper + 1) * LANES] * sign_u
            below = x[part, lower * LANES : (lower + 1) * LANES] * sign_l
            below = jnp.concatenate([below[8 * t : 8 * t + 8] for t in range(15, -1, -1)], axis=0)
            fold[part, 0, sl] = above + below
            fold[part, 1, sl] = above - below
            peak = jnp.maximum(peak, jnp.maximum(jnp.abs(above), jnp.abs(below)))
    peak = jnp.maximum(jnp.max(peak, axis=0, keepdims=True), 1e-30)
    scale = 65536.0 / peak
    unscale = peak * (1.0 / 65536.0)

    def convert(i):
        pick = pl.ds(i, HALF, stride=INNER)
        quarters = (
            (fold[0, 0, pick] * scale, 0, 0),
            (fold[1, 0, pick] * scale, 0, LANES),
            (fold[1, 1, pick] * scale, HALF, 0),
            (fold[0, 1, pick] * -scale, HALF, LANES),
        )
        for value, row, lane in quarters:
            high = value.astype(jnp.bfloat16)
            lanes = slice(lane, lane + LANES)
            rhs_h[i, row : row + HALF, lanes] = high
            rhs_l[i, row : row + HALF, lanes] = (value - high.astype(jnp.float32)).astype(FINE)
            rhs_l[i, DEPTH + row : DEPTH + row + HALF, lanes] = (value * (1.0 / STEP)).astype(FINE)

    convert(INNER - 1)

    def work(group, refs):
        blocks = GROUPS[group]
        start = rows_before(group)
        count = sum(size(half) for half, _ in blocks)
        tiles = []
        if group + 1 < len(GROUPS):
            row = start + count
            for half, d in GROUPS[group + 1]:
                first = source(half, d)
                for t in range(0, size(half), TILE):
                    tiles.append((pl.multiple_of(first + t, TILE), row + t))
                row += size(half)
        for step in range(INNER):
            i = INNER - 1 - step
            product = jnp.dot(
                lhs_h[start : start + count], rhs_h[i], preferred_element_type=jnp.float32
            ) + jnp.dot(
                lhs_l[start : start + count], rhs_l[i], preferred_element_type=jnp.float32
            )
            if group == 0 and i:
                convert(i - 1)
            for first, row in tiles[len(tiles) * step // INNER : len(tiles) * (step + 1) // INNER]:
                table_tile(first, row)
            first = 0
            for (half, d), ref in zip(blocks, refs):
                mine = slice(first, first + size(half))
                first += size(half)
                sl = pl.ds(source(half, d), size(half))
                new_real, new_imag = product[mine, :LANES], product[mine, LANES:]
                if step:
                    real, imag = acc[mine, :LANES], acc[mine, LANES:]
                    cos, sin = w[0, sl], w[1, sl]
                    new_real = real * cos + imag * sin + new_real
                    new_imag = imag * cos - real * sin + new_imag
                if i:
                    acc[mine, :LANES] = new_real
                    acc[mine, LANES:] = new_imag
                else:
                    cos, sin = pre[0, sl], pre[1, sl]
                    ref[:, :LANES] = (new_real * cos + new_imag * sin) * unscale
                    ref[:, LANES:] = (new_imag * cos - new_real * sin) * unscale

    sent = []

    def send(src, dst, sems, device):
        copy = pltpu.make_async_remote_copy(
            src_ref=src, dst_ref=dst, send_sem=sems[0], recv_sem=sems[1],
            device_id=device, device_id_type=MESH,
        )
        copy.start()
        sent.append(copy)
        return copy

    first_half = pl.ds(0, BLOCK_A // 2)
    second_half = pl.ds(BLOCK_A // 2, BLOCK_A // 2)
    whole = slice(None)

    def send_a(slot, out, to, part=whole):
        return send(
            a_out.at[out, part], a_in.at[slot, part], (a_send.at[slot], a_recv.at[slot]), at_z(to)
        )

    def send_b(d):
        slot = d % RING_Y - 1
        return send(b_out.at[slot], b_in.at[slot], (b_send.at[slot], b_recv.at[slot]), at_y(d))

    work(0, [a_out.at[0], a_out.at[1], b_out.at[1]])
    pl.semaphore_wait(barrier, len(partners))
    near = [send_a(0, 0, 1), send_a(1, 1, -1)]
    last_b = [send_b(2)]
    work(1, [a_out.at[2], b_out.at[0]])
    far = [send_a(2, 2, 2, first_half), send_a(3, 2, -2, second_half)]
    last_b.append(send_b(1))
    work(2, [a_out.at[3], a_out.at[4], b_out.at[2]])
    last_a = [send_a(4, 3, 1), send_a(5, 4, -1)]
    last_b.append(send_b(-1))
    work(3, [a_out.at[5], a_out.at[6]])
    for way, part in enumerate((first_half, second_half)):
        near[way].wait_recv()
        a_out[5 + way] += a_in[way]
        far[way].wait_recv()
        a_out[5 + way, part] += a_in[2 + way, part]
        last_a.append(send_a(6 + way, 5 + way, 2 - 4 * way))
    work(4, [sum_b, sum_a])

    def own(ref, place):
        return ref.at[pl.ds(pl.multiple_of(place * PART, PART), PART)]

    for copy in last_b:
        copy.wait_recv()
    sum_b[...] += b_in[0] + b_in[1] + b_in[2]
    copies_b = [
        send(
            own(sum_b, (z_here + d) % RING_Z), zb_in.at[d - 1],
            (zb_send.at[d - 1], zb_recv.at[d - 1]), at_z(d),
        )
        for d in range(1, RING_Z)
    ]
    for copy in last_a:
        copy.wait_recv()
    sum_a[...] += (a_in[4] + a_in[5]) + (a_in[6] + a_in[7])
    copies_a = [
        send(
            own(sum_a, (y_here + d) % RING_Y), ya_in.at[d - 1],
            (ya_send.at[d - 1], ya_recv.at[d - 1]), at_y(d),
        )
        for d in range(1, RING_Y)
    ]
    raw_b = own(sum_b, z_here)[...]
    for d, copy in enumerate(copies_b):
        copy.wait_recv()
        raw_b = raw_b + zb_in[d]
    raw_a = own(sum_a, y_here)[...]
    for d, copy in enumerate(copies_a):
        copy.wait_recv()
        raw_a = raw_a + ya_in[d]
    raw = jnp.concatenate([raw_a, raw_b], axis=0)

    real, imag = raw[:, :LANES], raw[:, LANES:]
    pad[...] = jnp.zeros_like(pad)
    pad[:OWN] = real * real + imag * imag
    total = jnp.sum(pad[...].T, axis=0, keepdims=True)
    energy[...] = jnp.broadcast_to(total, energy.shape)
    copies = [
        send(energy, n_in.at[d - 1], (n_send.at[d - 1], n_recv.at[d - 1]), at_panel(d))
        for d in range(1, PANELS)
    ]
    for d, copy in enumerate(copies):
        copy.wait_recv()
        total = total + n_in[d, :1]
    scale = lax.rsqrt(total * (1.0 / (LANES * PANELS)) + 1e-06)
    scale = jnp.broadcast_to(scale, (LANES, LANES)).T[:OWN]
    out_ref[:, 0] = real * scale
    out_ref[:, 1] = imag * scale
    for copy in sent:
        copy.wait_send()


def fused(green_matrix, sign_bits, picks):
    f32, bf16 = jnp.float32, jnp.bfloat16
    wide = 2 * LANES
    return pl.pallas_call(
        kernel,
        out_shape=jax.ShapeDtypeStruct((OWN, 2, LANES), f32),
        in_specs=[
            pl.BlockSpec(memory_space=pl.ANY),
            pl.BlockSpec(memory_space=pltpu.VMEM),
            pl.BlockSpec(memory_space=pltpu.VMEM),
        ],
        out_specs=pl.BlockSpec(memory_space=pltpu.VMEM),
        scratch_shapes=[
            pltpu.VMEM((2, LOCAL, LANES), f32),
            pltpu.VMEM((2, 2, LOCAL // 2, LANES), f32),
            pltpu.VMEM((INNER, DEPTH, wide), bf16),
            pltpu.VMEM((INNER, 2 * DEPTH, wide), FINE),
            pltpu.VMEM((SKETCH, DEPTH), bf16),
            pltpu.VMEM((SKETCH, 2 * DEPTH), FINE),
            pltpu.VMEM((3, SKETCH, LANES), f32),
            pltpu.VMEM((2, SKETCH, LANES), f32),
            pltpu.VMEM((2, SKETCH, LANES), f32),
            pltpu.VMEM((LANES, LANES), f32),
            pltpu.VMEM((2, LANES, LANES), f32),
            pltpu.VMEM((2 * BLOCK_A + BLOCK_B, wide), f32),
            pltpu.VMEM((BLOCK_A, wide), f32),
            pltpu.VMEM((BLOCK_B, wide), f32),
            pltpu.VMEM((7, BLOCK_A, wide), f32),
            pltpu.VMEM((8, BLOCK_A, wide), f32),
            pltpu.VMEM((RING_Y - 1, PART, wide), f32),
            pltpu.VMEM((RING_Y - 1, BLOCK_B, wide), f32),
            pltpu.VMEM((RING_Y - 1, BLOCK_B, wide), f32),
            pltpu.VMEM((RING_Z - 1, PART, wide), f32),
            pltpu.VMEM((8, LANES), f32),
            pltpu.VMEM((PANELS - 1, 8, LANES), f32),
            pltpu.SemaphoreType.DMA((8,)),
            pltpu.SemaphoreType.DMA((8,)),
            pltpu.SemaphoreType.DMA((8,)),
            pltpu.SemaphoreType.DMA((RING_Y - 1,)),
            pltpu.SemaphoreType.DMA((RING_Y - 1,)),
            pltpu.SemaphoreType.DMA((RING_Y - 1,)),
            pltpu.SemaphoreType.DMA((RING_Y - 1,)),
            pltpu.SemaphoreType.DMA((RING_Z - 1,)),
            pltpu.SemaphoreType.DMA((RING_Z - 1,)),
            pltpu.SemaphoreType.DMA((PANELS - 1,)),
            pltpu.SemaphoreType.DMA((PANELS - 1,)),
        ],
        compiler_params=pltpu.CompilerParams(
            collective_id=0, has_side_effects=True, vmem_limit_bytes=56 * 1024 * 1024
        ),
    )(green_matrix, sign_bits, picks)


def body(green_matrix, sign_bits, column_picks):
    return fused(green_matrix, sign_bits, column_picks)


def solution(mesh):
    placed = (P(None, "emit", "panel"), P("emit"), P())
    return jax.shard_map(
        body, mesh=mesh, in_specs=placed, out_specs=P("emit", None, "panel"), check_vma=False
    )
```

```python
import math

import jax
import jax.numpy as jnp
from jax import lax
from jax.experimental import pallas as pl
from jax.experimental.pallas import tpu as pltpu
from jax.sharding import PartitionSpec as P

EMITTERS = 196608
SKETCH = 1536
LOCAL = 6144
INNER = 8
HALF = 384
DEPTH = 2 * HALF
LANES = 128
PICK_ROWS = SKETCH // LANES
SIGN_ROWS = LOCAL // LANES
RING_Z = 8
RING_Y = 4
PANELS = 8
OWN = SKETCH // (RING_Z * RING_Y)
CLASSES = (("a", 24), ("b", 16), ("b", 8))
TILE = 32
FINE = jnp.float8_e4m3fn
STEP = 512.0
PLAN = (
    (((0, 4),), ((0, 4),)),
    (((1, 2), (0, 3), (0, -3),), ((0, 3), (0, -3), (1, 2),)),
    (((0, 1), (0, -1), (1, 1),), ((0, 1), (0, -1), (1, 1),)),
    (((1, -1),), ((1, -1),)),
    (((0, 2), (0, -2),), ((0, 2), (0, -2),)),
    (((2, 2),), ((2, 2),)),
    (((2, -1), (2, 1),), ((2, 1), (2, -1),)),
    (((1, 0), (0, 0),), ((1, "own"),)),
    (((2, 0),), ((2, "own"), (0, "own"),)),
)
BEARER = {4: 2, 3: 2, 2: 0, 1: 0}
MESH = pl.DeviceIdType.MESH


def wrap(values, period):
    return values - period * jnp.round(values * (1.0 / period))


def cos_sin(residue, period):
    t = residue * (math.pi / (2.0 * period))
    s = t * t
    sin = t * (1.0 + s * (-1.0 / 6 + s * (1.0 / 120 + s * (-1.0 / 5040 + s * (1.0 / 362880)))))
    versin = s * (0.5 + s * (-1.0 / 24 + s * (1.0 / 720 + s * (-1.0 / 40320))))
    cos = 1.0 - versin
    sin, cos = 2.0 * sin * cos, 1.0 - 2.0 * sin * sin
    return 1.0 - 2.0 * sin * sin, 2.0 * sin * cos


def block_rows(c):
    kind, count = CLASSES[c]
    return count * (RING_Y if kind == "a" else RING_Z)


def first_of_owner(c):
    return sum(count for _, count in CLASSES[:c])


def class_row(c):
    return first_of_owner(c) * RING_Y * RING_Z


def table_row(column):
    owner, rest = divmod(column, OWN)
    y, z = divmod(owner, RING_Z)
    c = max(c for c in range(len(CLASSES)) if first_of_owner(c) <= rest)
    kind, count = CLASSES[c]
    rest = rest - first_of_owner(c)
    if kind == "a":
        return class_row(c) + (z * RING_Y + y) * count + rest
    return class_row(c) + (y * RING_Z + z) * count + rest


def rows_before(group):
    return sum(block_rows(c) for blocks, _ in PLAN[:group] for c, _ in blocks)


MOST = max(rows_before(g + 1) - rows_before(g) for g in range(len(PLAN)))


def kernel(
    x_hbm, sign_ref, pick_ref, out_ref,
    x, fold, rhs_h, rhs_l, lhs_h, lhs_l, kb, w, pre, pad, tr, acc, energy, n_in,
    x_sem, n_send, n_recv, out, into, second, total, sems,
):
    position = lax.axis_index("emit")
    panel = lax.axis_index("panel")
    y_here, z_here = position // RING_Z, position % RING_Z

    def at_z(d):
        return {"emit": y_here * RING_Z + (z_here + d) % RING_Z}

    def at_y(d):
        return {"emit": (y_here + d) % RING_Y * RING_Z + z_here}

    def at_panel(d):
        return {"panel": (panel + d) % PANELS}

    parts = 8
    rows = LOCAL // parts
    copies = {}
    for part in (3, 4, 2, 5, 1, 6, 0, 7):
        sl = pl.ds(part * rows, rows)
        copies[part] = pltpu.make_async_copy(x_hbm.at[:, sl], x.at[:, sl], x_sem.at[part])
        copies[part].start()

    barrier = pltpu.get_barrier_semaphore()
    partners = [at_z(d) for d in range(1, RING_Z)]
    partners += [at_y(d) for d in range(1, RING_Y)]
    partners += [at_panel(d) for d in range(1, PANELS)]
    for partner in partners:
        pl.semaphore_signal(barrier, inc=1, device_id=partner, device_id_type=MESH)

    pad[...] = jnp.zeros_like(pad)
    k = pick_ref[...].reshape(PICK_ROWS, LANES)
    kf = k.astype(jnp.float32)
    turn = 6144 * ((position * k) & 31) + 3068 * k
    turn = turn - EMITTERS * jnp.round(turn.astype(jnp.float32) * (1.0 / EMITTERS)).astype(jnp.int32)
    reduced = wrap(kf, 49152.0)
    w_cos, w_sin = cos_sin(wrap(kf, float(EMITTERS)), float(EMITTERS))
    p_cos, p_sin = cos_sin(turn.astype(jnp.float32), float(EMITTERS))
    r_cos, r_sin = cos_sin(wrap(reduced * 256.0, 49152.0), 49152.0)
    for slot, value in enumerate((reduced, w_cos, w_sin, p_cos, p_sin, r_cos, r_sin)):
        pad[slot * 16 : slot * 16 + PICK_ROWS] = value
    tr[0] = pad[...].T
    pad[0:SIGN_ROWS] = (2 * sign_ref[...].reshape(SIGN_ROWS, LANES) - 1).astype(jnp.float32)
    tr[1] = pad[...].T
    for q in range(PICK_ROWS):
        for slot, ref in enumerate(
            (kb.at[0], w.at[0], w.at[1], pre.at[0], pre.at[1], kb.at[1], kb.at[2])
        ):
            c = slot * 16 + q
            spread = jnp.broadcast_to(tr[0, :, c : c + 1], (LANES, LANES))
            for first in range(0, LANES, 8):
                row = table_row(q * LANES + first)
                ref[row : row + 8] = spread[first : first + 8]

    odd = (2 * lax.broadcasted_iota(jnp.int32, (TILE, LANES), 1) + 1).astype(jnp.float32)

    def source(c, d):
        if CLASSES[c][0] == "a":
            place = (z_here + d) % RING_Z
        else:
            place = (y_here + d) % RING_Y
        return pl.multiple_of(class_row(c) + place * block_rows(c), TILE)

    def table_tile(first, row):
        sl = pl.ds(first, TILE)
        to = pl.ds(row, TILE)
        cos, sin = cos_sin(wrap(kb[0, sl] * odd, 49152.0), 49152.0)
        r_cos, r_sin = kb[1, sl], kb[2, sl]
        for g in range(3):
            if g:
                cos, sin = cos * r_cos - sin * r_sin, sin * r_cos + cos * r_sin
            for base, value in ((0, cos), (HALF, sin)):
                high = value.astype(jnp.bfloat16)
                lane = base + g * LANES
                lhs_h[to, lane : lane + LANES] = high
                lhs_l[to, lane : lane + LANES] = value.astype(FINE)
                rest = (value - high.astype(jnp.float32)) * STEP
                lhs_l[to, DEPTH + lane : DEPTH + lane + LANES] = rest.astype(FINE)

    row = 0
    for c, d in PLAN[0][0]:
        first = source(c, d)

        @pl.loop(0, block_rows(c) // TILE)
        def _(t, first=first, row=row):
            table_tile(
                pl.multiple_of(first + t * TILE, TILE), pl.multiple_of(row + t * TILE, TILE)
            )

        row += block_rows(c)

    peak = jnp.zeros((LANES, LANES), jnp.float32)
    for upper in range(SIGN_ROWS // 2, SIGN_ROWS):
        lower = SIGN_ROWS - 1 - upper
        if upper * LANES % rows == 0:
            copies[upper * LANES // rows].wait()
            copies[lower * LANES // rows].wait()
        sign_u = jnp.broadcast_to(tr[1, :, upper : upper + 1], (LANES, LANES))
        sign_l = jnp.broadcast_to(tr[1, :, lower : lower + 1], (LANES, LANES))
        sl = slice((upper - SIGN_ROWS // 2) * LANES, (upper - SIGN_ROWS // 2 + 1) * LANES)
        for part in range(2):
            above = x[part, upper * LANES : (upper + 1) * LANES] * sign_u
            below = x[part, lower * LANES : (lower + 1) * LANES] * sign_l
            below = jnp.concatenate([below[8 * t : 8 * t + 8] for t in range(15, -1, -1)], axis=0)
            fold[part, 0, sl] = above + below
            fold[part, 1, sl] = above - below
            peak = jnp.maximum(peak, jnp.maximum(jnp.abs(above), jnp.abs(below)))
    peak = jnp.maximum(jnp.max(peak, axis=0, keepdims=True), 1e-30)
    scale = 65536.0 / peak
    unscale = peak * (1.0 / 65536.0)

    def convert(i):
        pick = pl.ds(i, HALF, stride=INNER)
        quarters = (
            (fold[0, 0, pick] * scale, 0, 0),
            (fold[1, 0, pick] * scale, 0, LANES),
            (fold[1, 1, pick] * scale, HALF, 0),
            (fold[0, 1, pick] * -scale, HALF, LANES),
        )
        for value, row, lane in quarters:
            high = value.astype(jnp.bfloat16)
            lanes = slice(lane, lane + LANES)
            rhs_h[i, row : row + HALF, lanes] = high
            rhs_l[i, row : row + HALF, lanes] = (value - high.astype(jnp.float32)).astype(FINE)
            rhs_l[i, DEPTH + row : DEPTH + row + HALF, lanes] = (value * (1.0 / STEP)).astype(FINE)

    convert(INNER - 1)

    def work(group, refs):
        blocks = PLAN[group][0]
        start = rows_before(group)
        count = rows_before(group + 1) - start
        tiles = []
        if group + 1 < len(PLAN):
            row = start + count
            for c, d in PLAN[group + 1][0]:
                first = source(c, d)
                for t in range(0, block_rows(c), TILE):
                    tiles.append((pl.multiple_of(first + t, TILE), row + t))
                row += block_rows(c)
        for step in range(INNER):
            i = INNER - 1 - step
            product = jnp.dot(
                lhs_h[start : start + count], rhs_h[i], preferred_element_type=jnp.float32
            ) + jnp.dot(
                lhs_l[start : start + count], rhs_l[i], preferred_element_type=jnp.float32
            )
            if group == 0 and i:
                convert(i - 1)
            for first, row in tiles[len(tiles) * step // INNER : len(tiles) * (step + 1) // INNER]:
                table_tile(first, row)
            first = 0
            for (c, d), ref in zip(blocks, refs):
                mine = slice(first, first + block_rows(c))
                first += block_rows(c)
                sl = pl.ds(source(c, d), block_rows(c))
                new_real, new_imag = product[mine, :LANES], product[mine, LANES:]
                if step:
                    real, imag = acc[mine, :LANES], acc[mine, LANES:]
                    cos, sin = w[0, sl], w[1, sl]
                    new_real = real * cos + imag * sin + new_real
                    new_imag = imag * cos - real * sin + new_imag
                if i:
                    acc[mine, :LANES] = new_real
                    acc[mine, LANES:] = new_imag
                else:
                    cos, sin = pre[0, sl], pre[1, sl]
                    ref[:, :LANES] = (new_real * cos + new_imag * sin) * unscale
                    ref[:, LANES:] = (new_imag * cos - new_real * sin) * unscale

    sent = []

    def send(src, dst, sems, device):
        copy = pltpu.make_async_remote_copy(
            src_ref=src, dst_ref=dst, send_sem=sems[0], recv_sem=sems[1],
            device_id=device, device_id_type=MESH,
        )
        copy.start()
        sent.append(copy)
        return copy

    whole = slice(None)
    sent_by = {}
    last = {}

    def out_ref_of(c, d):
        if d == 0:
            return total[c]
        if CLASSES[c][0] == "b":
            return out[c].at[d % RING_Y - 1]
        return out[c].at[7 if d == 4 else abs(d) - 1 + (0 if d > 0 else 3)]

    def half_of(c, way):
        half = block_rows(c) // 2
        return pl.ds(half * way, half)

    def collect(c, way, far, ref):
        for d in (4, 3, 2, 1):
            if BEARER[d] == far:
                part = half_of(c, way) if d == 4 else whole
                sent_by[c, d, way].wait_recv()
                ref[part] += into[c][2 * (d - 1) + way, part]

    def leave(c, d):
        kind, count = CLASSES[c]
        if d == "own":
            if kind == "a":
                for way in range(2):
                    collect(c, way, 0, total[c])
                here, ring, device = y_here, RING_Y, at_y
            else:
                for slot in range(RING_Y - 1):
                    sent_by[c, slot].wait_recv()
                total[c][...] += into[c][0] + into[c][1] + into[c][2]
                here, ring, device = z_here, RING_Z, at_z
            last[c] = []
            for away in range(1, ring):
                start = pl.multiple_of((here + away) % ring * count, count)
                last[c].append(
                    send(
                        total[c].at[pl.ds(start, count)], second[c].at[away - 1],
                        (sems[c][2].at[away - 1], sems[c][3].at[away - 1]), device(away),
                    )
                )
        elif kind == "b":
            slot = d % RING_Y - 1
            sent_by[c, slot] = send(
                out[c].at[slot], into[c].at[slot], (sems[c][0].at[slot], sems[c][1].at[slot]), at_y(d)
            )
        else:
            far = abs(d)
            hops = far - BEARER[far]
            for way in (0, 1) if d == 4 else (int(d < 0),):
                part = half_of(c, way) if d == 4 else whole
                ref = out_ref_of(c, d)
                if far < 4:
                    collect(c, way, far, ref)
                slot = 2 * (far - 1) + way
                sent_by[c, far, way] = send(
                    ref.at[part], into[c].at[slot, part],
                    (sems[c][0].at[slot], sems[c][1].at[slot]), at_z(hops - 2 * hops * way),
                )

    for g, (blocks, messages) in enumerate(PLAN):
        work(g, [out_ref_of(c, d) for c, d in blocks])
        if g == 0:
            pl.semaphore_wait(barrier, len(partners))
        for c, d in messages:
            leave(c, d)

    pieces = []
    for c, (kind, count) in enumerate(CLASSES):
        place = y_here if kind == "a" else z_here
        piece = total[c][pl.ds(pl.multiple_of(place * count, count), count)]
        for d, copy in enumerate(last[c]):
            copy.wait_recv()
            piece = piece + second[c][d]
        pieces.append(piece)
    raw = jnp.concatenate(pieces, axis=0)

    real, imag = raw[:, :LANES], raw[:, LANES:]
    pad[...] = jnp.zeros_like(pad)
    pad[:OWN] = real * real + imag * imag
    total = jnp.sum(pad[...].T, axis=0, keepdims=True)
    energy[...] = jnp.broadcast_to(total, energy.shape)
    copies = [
        send(energy, n_in.at[d - 1], (n_send.at[d - 1], n_recv.at[d - 1]), at_panel(d))
        for d in range(1, PANELS)
    ]
    for d, copy in enumerate(copies):
        copy.wait_recv()
        total = total + n_in[d, :1]
    scale = lax.rsqrt(total * (1.0 / (LANES * PANELS)) + 1e-06)
    scale = jnp.broadcast_to(scale, (LANES, LANES)).T[:OWN]
    out_ref[:, 0] = real * scale
    out_ref[:, 1] = imag * scale
    for copy in sent:
        copy.wait_send()


def fused(green_matrix, sign_bits, picks):
    f32, bf16 = jnp.float32, jnp.bfloat16
    wide = 2 * LANES
    return pl.pallas_call(
        kernel,
        out_shape=jax.ShapeDtypeStruct((OWN, 2, LANES), f32),
        in_specs=[
            pl.BlockSpec(memory_space=pl.ANY),
            pl.BlockSpec(memory_space=pltpu.VMEM),
            pl.BlockSpec(memory_space=pltpu.VMEM),
        ],
        out_specs=pl.BlockSpec(memory_space=pltpu.VMEM),
        scratch_shapes=[
            pltpu.VMEM((2, LOCAL, LANES), f32),
            pltpu.VMEM((2, 2, LOCAL // 2, LANES), f32),
            pltpu.VMEM((INNER, DEPTH, wide), bf16),
            pltpu.VMEM((INNER, 2 * DEPTH, wide), FINE),
            pltpu.VMEM((SKETCH, DEPTH), bf16),
            pltpu.VMEM((SKETCH, 2 * DEPTH), FINE),
            pltpu.VMEM((3, SKETCH, LANES), f32),
            pltpu.VMEM((2, SKETCH, LANES), f32),
            pltpu.VMEM((2, SKETCH, LANES), f32),
            pltpu.VMEM((LANES, LANES), f32),
            pltpu.VMEM((2, LANES, LANES), f32),
            pltpu.VMEM((MOST, wide), f32),
            pltpu.VMEM((8, LANES), f32),
            pltpu.VMEM((PANELS - 1, 8, LANES), f32),
            pltpu.SemaphoreType.DMA((8,)),
            pltpu.SemaphoreType.DMA((PANELS - 1,)),
            pltpu.SemaphoreType.DMA((PANELS - 1,)),
            [pltpu.VMEM((8 if kind == "a" else 3, block_rows(c), wide), f32) for c, (kind, _) in enumerate(CLASSES)],
            [pltpu.VMEM((8 if kind == "a" else 3, block_rows(c), wide), f32) for c, (kind, _) in enumerate(CLASSES)],
            [pltpu.VMEM((RING_Z - 1, count, wide), f32) for _, count in CLASSES],
            [pltpu.VMEM((block_rows(c), wide), f32) for c in range(len(CLASSES))],
            [[pltpu.SemaphoreType.DMA((8,))] * 4 for _ in CLASSES],
        ],
        compiler_params=pltpu.CompilerParams(
            collective_id=0, has_side_effects=True, vmem_limit_bytes=56 * 1024 * 1024
        ),
    )(green_matrix, sign_bits, picks)


def body(green_matrix, sign_bits, column_picks):
    return fused(green_matrix, sign_bits, column_picks)


def solution(mesh):
    placed = (P(None, "emit", "panel"), P("emit"), P())
    return jax.shard_map(
        body, mesh=mesh, in_specs=placed, out_specs=P("emit", None, "panel"), check_vma=False
    )
```

```python
import math

import jax
import jax.numpy as jnp
from jax import lax
from jax.experimental import pallas as pl
from jax.experimental.pallas import tpu as pltpu
from jax.sharding import PartitionSpec as P

EMITTERS = 196608
SKETCH = 1536
LOCAL = 6144
INNER = 8
HALF = 384
DEPTH = 2 * HALF
LANES = 128
PICK_ROWS = SKETCH // LANES
SIGN_ROWS = LOCAL // LANES
RING_Z = 8
RING_Y = 4
PANELS = 8
OWN = SKETCH // (RING_Z * RING_Y)
CLASSES = (("a", 24), ("b", 16), ("b", 8))
TILE = 32
FINE = jnp.float8_e4m3fn
STEP = 512.0
PLAN = (
    (((0, 4), (0, 3), (0, -3),), ((0, 4), (0, 3), (0, -3),)),
    (((1, 2),), ((1, 2),)),
    (((0, 1), (0, -1), (1, 1),), ((0, 1), (0, -1), (1, 1),)),
    (((1, -1),), ((1, -1),)),
    (((0, 2), (0, -2),), ((0, 2), (0, -2),)),
    (((2, 2),), ((2, 2),)),
    (((2, 1), (2, -1),), ((2, 1), (2, -1),)),
    (((1, 0), (0, 0),), ((1, "own"),)),
    (((2, 0),), ((2, "own"), (0, "own"),)),
)
BEARER = {4: 2, 3: 2, 2: 0, 1: 0}
MESH = pl.DeviceIdType.MESH


def wrap(values, period):
    return values - period * jnp.round(values * (1.0 / period))


def cos_sin(residue, period):
    t = residue * (math.pi / (2.0 * period))
    s = t * t
    sin = t * (1.0 + s * (-1.0 / 6 + s * (1.0 / 120 + s * (-1.0 / 5040 + s * (1.0 / 362880)))))
    versin = s * (0.5 + s * (-1.0 / 24 + s * (1.0 / 720 + s * (-1.0 / 40320))))
    cos = 1.0 - versin
    sin, cos = 2.0 * sin * cos, 1.0 - 2.0 * sin * sin
    return 1.0 - 2.0 * sin * sin, 2.0 * sin * cos


def block_rows(c):
    kind, count = CLASSES[c]
    return count * (RING_Y if kind == "a" else RING_Z)


def first_of_owner(c):
    return sum(count for _, count in CLASSES[:c])


def class_row(c):
    return first_of_owner(c) * RING_Y * RING_Z


def table_row(column):
    owner, rest = divmod(column, OWN)
    y, z = divmod(owner, RING_Z)
    c = max(c for c in range(len(CLASSES)) if first_of_owner(c) <= rest)
    kind, count = CLASSES[c]
    rest = rest - first_of_owner(c)
    if kind == "a":
        return class_row(c) + (z * RING_Y + y) * count + rest
    return class_row(c) + (y * RING_Z + z) * count + rest


def rows_before(group):
    return sum(block_rows(c) for blocks, _ in PLAN[:group] for c, _ in blocks)


MOST = max(rows_before(g + 1) - rows_before(g) for g in range(len(PLAN)))


def kernel(
    x_hbm, sign_ref, pick_ref, out_ref,
    x, fold, rhs_h, rhs_l, lhs_h, lhs_l, kb, w, pre, pad, tr, acc, energy, n_in,
    x_sem, n_send, n_recv, out, into, second, total, sems,
):
    position = lax.axis_index("emit")
    panel = lax.axis_index("panel")
    y_here, z_here = position // RING_Z, position % RING_Z

    def at_z(d):
        return {"emit": y_here * RING_Z + (z_here + d) % RING_Z}

    def at_y(d):
        return {"emit": (y_here + d) % RING_Y * RING_Z + z_here}

    def at_panel(d):
        return {"panel": (panel + d) % PANELS}

    parts = 8
    rows = LOCAL // parts
    copies = {}
    for part in (3, 4, 2, 5, 1, 6, 0, 7):
        sl = pl.ds(part * rows, rows)
        copies[part] = pltpu.make_async_copy(x_hbm.at[:, sl], x.at[:, sl], x_sem.at[part])
        copies[part].start()

    barrier = pltpu.get_barrier_semaphore()
    partners = [at_z(d) for d in range(1, RING_Z)]
    partners += [at_y(d) for d in range(1, RING_Y)]
    partners += [at_panel(d) for d in range(1, PANELS)]
    for partner in partners:
        pl.semaphore_signal(barrier, inc=1, device_id=partner, device_id_type=MESH)

    pad[...] = jnp.zeros_like(pad)
    k = pick_ref[...].reshape(PICK_ROWS, LANES)
    kf = k.astype(jnp.float32)
    turn = 6144 * ((position * k) & 31) + 3068 * k
    turn = turn - EMITTERS * jnp.round(turn.astype(jnp.float32) * (1.0 / EMITTERS)).astype(jnp.int32)
    reduced = wrap(kf, 49152.0)
    w_cos, w_sin = cos_sin(wrap(kf, float(EMITTERS)), float(EMITTERS))
    p_cos, p_sin = cos_sin(turn.astype(jnp.float32), float(EMITTERS))
    r_cos, r_sin = cos_sin(wrap(reduced * 256.0, 49152.0), 49152.0)
    for slot, value in enumerate((reduced, w_cos, w_sin, p_cos, p_sin, r_cos, r_sin)):
        pad[slot * 16 : slot * 16 + PICK_ROWS] = value
    tr[0] = pad[...].T
    pad[0:SIGN_ROWS] = (2 * sign_ref[...].reshape(SIGN_ROWS, LANES) - 1).astype(jnp.float32)
    tr[1] = pad[...].T
    for q in range(PICK_ROWS):
        for slot, ref in enumerate(
            (kb.at[0], w.at[0], w.at[1], pre.at[0], pre.at[1], kb.at[1], kb.at[2])
        ):
            c = slot * 16 + q
            spread = jnp.broadcast_to(tr[0, :, c : c + 1], (LANES, LANES))
            for first in range(0, LANES, 8):
                row = table_row(q * LANES + first)
                ref[row : row + 8] = spread[first : first + 8]

    odd = (2 * lax.broadcasted_iota(jnp.int32, (TILE, LANES), 1) + 1).astype(jnp.float32)

    def source(c, d):
        if CLASSES[c][0] == "a":
            place = (z_here + d) % RING_Z
        else:
            place = (y_here + d) % RING_Y
        return pl.multiple_of(class_row(c) + place * block_rows(c), TILE)

    def table_tile(first, row):
        sl = pl.ds(first, TILE)
        to = pl.ds(row, TILE)
        cos, sin = cos_sin(wrap(kb[0, sl] * odd, 49152.0), 49152.0)
        r_cos, r_sin = kb[1, sl], kb[2, sl]
        for g in range(3):
            if g:
                cos, sin = cos * r_cos - sin * r_sin, sin * r_cos + cos * r_sin
            for base, value in ((0, cos), (HALF, sin)):
                high = value.astype(jnp.bfloat16)
                lane = base + g * LANES
                lhs_h[to, lane : lane + LANES] = high
                lhs_l[to, lane : lane + LANES] = value.astype(FINE)
                rest = (value - high.astype(jnp.float32)) * STEP
                lhs_l[to, DEPTH + lane : DEPTH + lane + LANES] = rest.astype(FINE)

    row = 0
    for c, d in PLAN[0][0]:
        first = source(c, d)

        @pl.loop(0, block_rows(c) // TILE)
        def _(t, first=first, row=row):
            table_tile(
                pl.multiple_of(first + t * TILE, TILE), pl.multiple_of(row + t * TILE, TILE)
            )

        row += block_rows(c)

    peak = jnp.zeros((LANES, LANES), jnp.float32)
    for upper in range(SIGN_ROWS // 2, SIGN_ROWS):
        lower = SIGN_ROWS - 1 - upper
        if upper * LANES % rows == 0:
            copies[upper * LANES // rows].wait()
            copies[lower * LANES // rows].wait()
        sign_u = jnp.broadcast_to(tr[1, :, upper : upper + 1], (LANES, LANES))
        sign_l = jnp.broadcast_to(tr[1, :, lower : lower + 1], (LANES, LANES))
        sl = slice((upper - SIGN_ROWS // 2) * LANES, (upper - SIGN_ROWS // 2 + 1) * LANES)
        for part in range(2):
            above = x[part, upper * LANES : (upper + 1) * LANES] * sign_u
            below = x[part, lower * LANES : (lower + 1) * LANES] * sign_l
            below = jnp.concatenate([below[8 * t : 8 * t + 8] for t in range(15, -1, -1)], axis=0)
            fold[part, 0, sl] = above + below
            fold[part, 1, sl] = above - below
            peak = jnp.maximum(peak, jnp.maximum(jnp.abs(above), jnp.abs(below)))
    peak = jnp.maximum(jnp.max(peak, axis=0, keepdims=True), 1e-30)
    scale = 65536.0 / peak
    unscale = peak * (1.0 / 65536.0)

    def convert(i):
        pick = pl.ds(i, HALF, stride=INNER)
        quarters = (
            (fold[0, 0, pick] * scale, 0, 0),
            (fold[1, 0, pick] * scale, 0, LANES),
            (fold[1, 1, pick] * scale, HALF, 0),
            (fold[0, 1, pick] * -scale, HALF, LANES),
        )
        for value, row, lane in quarters:
            high = value.astype(jnp.bfloat16)
            lanes = slice(lane, lane + LANES)
            rhs_h[i, row : row + HALF, lanes] = high
            rhs_l[i, row : row + HALF, lanes] = (value - high.astype(jnp.float32)).astype(FINE)
            rhs_l[i, DEPTH + row : DEPTH + row + HALF, lanes] = (value * (1.0 / STEP)).astype(FINE)

    convert(INNER - 1)

    def work(group, refs):
        blocks = PLAN[group][0]
        start = rows_before(group)
        count = rows_before(group + 1) - start
        tiles = []
        if group + 1 < len(PLAN):
            row = start + count
            for c, d in PLAN[group + 1][0]:
                first = source(c, d)
                for t in range(0, block_rows(c), TILE):
                    tiles.append((pl.multiple_of(first + t, TILE), row + t))
                row += block_rows(c)
        for step in range(INNER):
            i = INNER - 1 - step
            product = jnp.dot(
                lhs_h[start : start + count], rhs_h[i], preferred_element_type=jnp.float32
            ) + jnp.dot(
                lhs_l[start : start + count], rhs_l[i], preferred_element_type=jnp.float32
            )
            if group == 0 and i:
                convert(i - 1)
            for first, row in tiles[len(tiles) * step // INNER : len(tiles) * (step + 1) // INNER]:
                table_tile(first, row)
            first = 0
            for (c, d), ref in zip(blocks, refs):
                mine = slice(first, first + block_rows(c))
                first += block_rows(c)
                sl = pl.ds(source(c, d), block_rows(c))
                new_real, new_imag = product[mine, :LANES], product[mine, LANES:]
                if step:
                    real, imag = acc[mine, :LANES], acc[mine, LANES:]
                    cos, sin = w[0, sl], w[1, sl]
                    new_real = real * cos + imag * sin + new_real
                    new_imag = imag * cos - real * sin + new_imag
                if i:
                    acc[mine, :LANES] = new_real
                    acc[mine, LANES:] = new_imag
                else:
                    cos, sin = pre[0, sl], pre[1, sl]
                    ref[:, :LANES] = (new_real * cos + new_imag * sin) * unscale
                    ref[:, LANES:] = (new_imag * cos - new_real * sin) * unscale

    sent = []

    def send(src, dst, sems, device):
        copy = pltpu.make_async_remote_copy(
            src_ref=src, dst_ref=dst, send_sem=sems[0], recv_sem=sems[1],
            device_id=device, device_id_type=MESH,
        )
        copy.start()
        sent.append(copy)
        return copy

    whole = slice(None)
    sent_by = {}
    last = {}

    def out_ref_of(c, d):
        if d == 0:
            return total[c]
        if CLASSES[c][0] == "b":
            return out[c].at[d % RING_Y - 1]
        return out[c].at[7 if d == 4 else abs(d) - 1 + (0 if d > 0 else 3)]

    def half_of(c, way):
        half = block_rows(c) // 2
        return pl.ds(half * way, half)

    def collect(c, way, far, ref):
        for d in (4, 3, 2, 1):
            if BEARER[d] == far:
                part = half_of(c, way) if d == 4 else whole
                sent_by[c, d, way].wait_recv()
                ref[part] += into[c][2 * (d - 1) + way, part]

    def leave(c, d):
        kind, count = CLASSES[c]
        if d == "own":
            if kind == "a":
                for way in range(2):
                    collect(c, way, 0, total[c])
                here, ring, device = y_here, RING_Y, at_y
            else:
                for slot in range(RING_Y - 1):
                    sent_by[c, slot].wait_recv()
                total[c][...] += into[c][0] + into[c][1] + into[c][2]
                here, ring, device = z_here, RING_Z, at_z
            last[c] = []
            for away in range(1, ring):
                start = pl.multiple_of((here + away) % ring * count, count)
                last[c].append(
                    send(
                        total[c].at[pl.ds(start, count)], second[c].at[away - 1],
                        (sems[c][2].at[away - 1], sems[c][3].at[away - 1]), device(away),
                    )
                )
        elif kind == "b":
            slot = d % RING_Y - 1
            sent_by[c, slot] = send(
                out[c].at[slot], into[c].at[slot], (sems[c][0].at[slot], sems[c][1].at[slot]), at_y(d)
            )
        else:
            far = abs(d)
            hops = far - BEARER[far]
            for way in (0, 1) if d == 4 else (int(d < 0),):
                part = half_of(c, way) if d == 4 else whole
                ref = out_ref_of(c, d)
                if far < 4:
                    collect(c, way, far, ref)
                slot = 2 * (far - 1) + way
                sent_by[c, far, way] = send(
                    ref.at[part], into[c].at[slot, part],
                    (sems[c][0].at[slot], sems[c][1].at[slot]), at_z(hops - 2 * hops * way),
                )

    for g, (blocks, messages) in enumerate(PLAN):
        work(g, [out_ref_of(c, d) for c, d in blocks])
        if g == 0:
            pl.semaphore_wait(barrier, len(partners))
        for c, d in messages:
            leave(c, d)

    pieces = []
    for c, (kind, count) in enumerate(CLASSES):
        place = y_here if kind == "a" else z_here
        piece = total[c][pl.ds(pl.multiple_of(place * count, count), count)]
        for d, copy in enumerate(last[c]):
            copy.wait_recv()
            piece = piece + second[c][d]
        pieces.append(piece)
    raw = jnp.concatenate(pieces, axis=0)

    real, imag = raw[:, :LANES], raw[:, LANES:]
    pad[...] = jnp.zeros_like(pad)
    pad[:OWN] = real * real + imag * imag
    total = jnp.sum(pad[...].T, axis=0, keepdims=True)
    energy[...] = jnp.broadcast_to(total, energy.shape)
    copies = [
        send(energy, n_in.at[d - 1], (n_send.at[d - 1], n_recv.at[d - 1]), at_panel(d))
        for d in range(1, PANELS)
    ]
    for d, copy in enumerate(copies):
        copy.wait_recv()
        total = total + n_in[d, :1]
    scale = lax.rsqrt(total * (1.0 / (LANES * PANELS)) + 1e-06)
    scale = jnp.broadcast_to(scale, (LANES, LANES)).T[:OWN]
    out_ref[:, 0] = real * scale
    out_ref[:, 1] = imag * scale
    for copy in sent:
        copy.wait_send()


def fused(green_matrix, sign_bits, picks):
    f32, bf16 = jnp.float32, jnp.bfloat16
    wide = 2 * LANES
    return pl.pallas_call(
        kernel,
        out_shape=jax.ShapeDtypeStruct((OWN, 2, LANES), f32),
        in_specs=[
            pl.BlockSpec(memory_space=pl.ANY),
            pl.BlockSpec(memory_space=pltpu.VMEM),
            pl.BlockSpec(memory_space=pltpu.VMEM),
        ],
        out_specs=pl.BlockSpec(memory_space=pltpu.VMEM),
        scratch_shapes=[
            pltpu.VMEM((2, LOCAL, LANES), f32),
            pltpu.VMEM((2, 2, LOCAL // 2, LANES), f32),
            pltpu.VMEM((INNER, DEPTH, wide), bf16),
            pltpu.VMEM((INNER, 2 * DEPTH, wide), FINE),
            pltpu.VMEM((SKETCH, DEPTH), bf16),
            pltpu.VMEM((SKETCH, 2 * DEPTH), FINE),
            pltpu.VMEM((3, SKETCH, LANES), f32),
            pltpu.VMEM((2, SKETCH, LANES), f32),
            pltpu.VMEM((2, SKETCH, LANES), f32),
            pltpu.VMEM((LANES, LANES), f32),
            pltpu.VMEM((2, LANES, LANES), f32),
            pltpu.VMEM((MOST, wide), f32),
            pltpu.VMEM((8, LANES), f32),
            pltpu.VMEM((PANELS - 1, 8, LANES), f32),
            pltpu.SemaphoreType.DMA((8,)),
            pltpu.SemaphoreType.DMA((PANELS - 1,)),
            pltpu.SemaphoreType.DMA((PANELS - 1,)),
            [pltpu.VMEM((8 if kind == "a" else 3, block_rows(c), wide), f32) for c, (kind, _) in enumerate(CLASSES)],
            [pltpu.VMEM((8 if kind == "a" else 3, block_rows(c), wide), f32) for c, (kind, _) in enumerate(CLASSES)],
            [pltpu.VMEM((RING_Z - 1, count, wide), f32) for _, count in CLASSES],
            [pltpu.VMEM((block_rows(c), wide), f32) for c in range(len(CLASSES))],
            [[pltpu.SemaphoreType.DMA((8,))] * 4 for _ in CLASSES],
        ],
        compiler_params=pltpu.CompilerParams(
            collective_id=0, has_side_effects=True, vmem_limit_bytes=56 * 1024 * 1024
        ),
    )(green_matrix, sign_bits, picks)


def body(green_matrix, sign_bits, column_picks):
    return fused(green_matrix, sign_bits, column_picks)


def solution(mesh):
    placed = (P(None, "emit", "panel"), P("emit"), P())
    return jax.shard_map(
        body, mesh=mesh, in_specs=placed, out_specs=P("emit", None, "panel"), check_vma=False
    )
```

```python
import math

import jax
import jax.numpy as jnp
from jax import lax
from jax.experimental import pallas as pl
from jax.experimental.pallas import tpu as pltpu
from jax.sharding import PartitionSpec as P

EMITTERS = 196608
SKETCH = 1536
LOCAL = 6144
INNER = 8
HALF = 384
DEPTH = 2 * HALF
LANES = 128
PICK_ROWS = SKETCH // LANES
SIGN_ROWS = LOCAL // LANES
RING_Z = 8
RING_Y = 4
PANELS = 8
OWN = SKETCH // (RING_Z * RING_Y)
CLASSES = (("a", 24), ("b", 16), ("b", 8))
TILE = 32
FINE = jnp.float8_e4m3fn
STEP = 512.0
PLAN = (
    (((0, 4), (0, 3), (0, -3),), ((0, 4), (0, 3), (0, -3),)),
    (((1, 2),), ((1, 2),)),
    (((0, 1), (0, -1), (1, 1),), ((0, 1), (0, -1), (1, 1),)),
    (((1, -1),), ((1, -1),)),
    (((0, 2), (0, -2),), ((0, 2), (0, -2),)),
    (((2, 2),), ((2, 2),)),
    (((2, 1), (2, -1),), ((2, 1), (2, -1),)),
    (((1, 0), (0, 0),), ((1, "own"),)),
    (((2, 0),), ((2, "own"), (0, "own"),)),
)
BEARER = {4: 2, 3: 2, 2: 0, 1: 0}
MESH = pl.DeviceIdType.MESH


def wrap(values, period):
    return values - period * jnp.round(values * (1.0 / period))


def cos_sin(residue, period):
    t = residue * (math.pi / (2.0 * period))
    s = t * t
    sin = t * (1.0 + s * (-1.0 / 6 + s * (1.0 / 120 + s * (-1.0 / 5040 + s * (1.0 / 362880)))))
    versin = s * (0.5 + s * (-1.0 / 24 + s * (1.0 / 720 + s * (-1.0 / 40320))))
    cos = 1.0 - versin
    sin, cos = 2.0 * sin * cos, 1.0 - 2.0 * sin * sin
    return 1.0 - 2.0 * sin * sin, 2.0 * sin * cos


def block_rows(c):
    kind, count = CLASSES[c]
    return count * (RING_Y if kind == "a" else RING_Z)


def first_of_owner(c):
    return sum(count for _, count in CLASSES[:c])


def class_row(c):
    return first_of_owner(c) * RING_Y * RING_Z


def table_row(column):
    owner, rest = divmod(column, OWN)
    y, z = divmod(owner, RING_Z)
    c = max(c for c in range(len(CLASSES)) if first_of_owner(c) <= rest)
    kind, count = CLASSES[c]
    rest = rest - first_of_owner(c)
    if kind == "a":
        return class_row(c) + (z * RING_Y + y) * count + rest
    return class_row(c) + (y * RING_Z + z) * count + rest


def rows_before(group):
    return sum(block_rows(c) for blocks, _ in PLAN[:group] for c, _ in blocks)


MOST = max(rows_before(g + 1) - rows_before(g) for g in range(len(PLAN)))


def kernel(
    x_hbm, sign_ref, pick_ref, out_ref,
    x, fold, rhs_h, rhs_l, lhs_h, lhs_l, kb, w, pre, pad, tr, acc, energy, n_in,
    x_sem, n_send, n_recv, out, into, second, total, sems,
):
    position = lax.axis_index("emit")
    panel = lax.axis_index("panel")
    y_here, z_here = position // RING_Z, position % RING_Z

    def at_z(d):
        return {"emit": y_here * RING_Z + (z_here + d) % RING_Z}

    def at_y(d):
        return {"emit": (y_here + d) % RING_Y * RING_Z + z_here}

    def at_panel(d):
        return {"panel": (panel + d) % PANELS}

    parts = 8
    rows = LOCAL // parts
    copies = {}
    for part in (3, 4, 2, 5, 1, 6, 0, 7):
        sl = pl.ds(part * rows, rows)
        copies[part] = pltpu.make_async_copy(x_hbm.at[:, sl], x.at[:, sl], x_sem.at[part])
        copies[part].start()

    barrier = pltpu.get_barrier_semaphore()
    partners = [at_z(d) for d in range(1, RING_Z)]
    partners += [at_y(d) for d in range(1, RING_Y)]
    partners += [at_panel(d) for d in range(1, PANELS)]
    for partner in partners:
        pl.semaphore_signal(barrier, inc=1, device_id=partner, device_id_type=MESH)

    pad[...] = jnp.zeros_like(pad)
    k = pick_ref[...].reshape(PICK_ROWS, LANES)
    kf = k.astype(jnp.float32)
    turn = 6144 * ((position * k) & 31) + 3068 * k
    turn = turn - EMITTERS * jnp.round(turn.astype(jnp.float32) * (1.0 / EMITTERS)).astype(jnp.int32)
    reduced = wrap(kf, 49152.0)
    w_cos, w_sin = cos_sin(wrap(kf, float(EMITTERS)), float(EMITTERS))
    p_cos, p_sin = cos_sin(turn.astype(jnp.float32), float(EMITTERS))
    r_cos, r_sin = cos_sin(wrap(reduced * 256.0, 49152.0), 49152.0)
    for slot, value in enumerate((reduced, w_cos, w_sin, p_cos, p_sin, r_cos, r_sin)):
        pad[slot * 16 : slot * 16 + PICK_ROWS] = value
    tr[0] = pad[...].T
    pad[0:SIGN_ROWS] = (2 * sign_ref[...].reshape(SIGN_ROWS, LANES) - 1).astype(jnp.float32)
    tr[1] = pad[...].T
    pad[...] = jnp.zeros_like(pad)
    for q in range(PICK_ROWS):
        for slot, ref in enumerate(
            (kb.at[0], w.at[0], w.at[1], pre.at[0], pre.at[1], kb.at[1], kb.at[2])
        ):
            c = slot * 16 + q
            spread = jnp.broadcast_to(tr[0, :, c : c + 1], (LANES, LANES))
            for first in range(0, LANES, 8):
                row = table_row(q * LANES + first)
                ref[row : row + 8] = spread[first : first + 8]

    odd = (2 * lax.broadcasted_iota(jnp.int32, (TILE, LANES), 1) + 1).astype(jnp.float32)

    def source(c, d):
        if CLASSES[c][0] == "a":
            place = (z_here + d) % RING_Z
        else:
            place = (y_here + d) % RING_Y
        return pl.multiple_of(class_row(c) + place * block_rows(c), TILE)

    def table_tile(first, row):
        sl = pl.ds(first, TILE)
        to = pl.ds(row, TILE)
        cos, sin = cos_sin(wrap(kb[0, sl] * odd, 49152.0), 49152.0)
        r_cos, r_sin = kb[1, sl], kb[2, sl]
        for g in range(3):
            if g:
                cos, sin = cos * r_cos - sin * r_sin, sin * r_cos + cos * r_sin
            for base, value in ((0, cos), (HALF, sin)):
                high = value.astype(jnp.bfloat16)
                lane = base + g * LANES
                lhs_h[to, lane : lane + LANES] = high
                lhs_l[to, lane : lane + LANES] = value.astype(FINE)
                rest = (value - high.astype(jnp.float32)) * STEP
                lhs_l[to, DEPTH + lane : DEPTH + lane + LANES] = rest.astype(FINE)

    row = 0
    for c, d in PLAN[0][0]:
        first = source(c, d)

        @pl.loop(0, block_rows(c) // TILE)
        def _(t, first=first, row=row):
            table_tile(
                pl.multiple_of(first + t * TILE, TILE), pl.multiple_of(row + t * TILE, TILE)
            )

        row += block_rows(c)

    peak = jnp.zeros((LANES, LANES), jnp.float32)
    for upper in range(SIGN_ROWS // 2, SIGN_ROWS):
        lower = SIGN_ROWS - 1 - upper
        if upper * LANES % rows == 0:
            copies[upper * LANES // rows].wait()
            copies[lower * LANES // rows].wait()
        sign_u = jnp.broadcast_to(tr[1, :, upper : upper + 1], (LANES, LANES))
        sign_l = jnp.broadcast_to(tr[1, :, lower : lower + 1], (LANES, LANES))
        sl = slice((upper - SIGN_ROWS // 2) * LANES, (upper - SIGN_ROWS // 2 + 1) * LANES)
        for part in range(2):
            above = x[part, upper * LANES : (upper + 1) * LANES] * sign_u
            below = x[part, lower * LANES : (lower + 1) * LANES] * sign_l
            below = jnp.concatenate([below[8 * t : 8 * t + 8] for t in range(15, -1, -1)], axis=0)
            fold[part, 0, sl] = above + below
            fold[part, 1, sl] = above - below
            peak = jnp.maximum(peak, jnp.maximum(jnp.abs(above), jnp.abs(below)))
    peak = jnp.maximum(jnp.max(peak, axis=0, keepdims=True), 1e-30)
    scale = 65536.0 / peak
    unscale = peak * (1.0 / 65536.0)

    def convert(i):
        pick = pl.ds(i, HALF, stride=INNER)
        quarters = (
            (fold[0, 0, pick] * scale, 0, 0),
            (fold[1, 0, pick] * scale, 0, LANES),
            (fold[1, 1, pick] * scale, HALF, 0),
            (fold[0, 1, pick] * -scale, HALF, LANES),
        )
        for value, row, lane in quarters:
            high = value.astype(jnp.bfloat16)
            lanes = slice(lane, lane + LANES)
            rhs_h[i, row : row + HALF, lanes] = high
            rhs_l[i, row : row + HALF, lanes] = (value - high.astype(jnp.float32)).astype(FINE)
            rhs_l[i, DEPTH + row : DEPTH + row + HALF, lanes] = (value * (1.0 / STEP)).astype(FINE)

    convert(INNER - 1)

    def work(group, refs):
        blocks = PLAN[group][0]
        start = rows_before(group)
        count = rows_before(group + 1) - start
        tiles = []
        if group + 1 < len(PLAN):
            row = start + count
            for c, d in PLAN[group + 1][0]:
                first = source(c, d)
                for t in range(0, block_rows(c), TILE):
                    tiles.append((pl.multiple_of(first + t, TILE), row + t))
                row += block_rows(c)
        for step in range(INNER):
            i = INNER - 1 - step
            product = jnp.dot(
                lhs_h[start : start + count], rhs_h[i], preferred_element_type=jnp.float32
            ) + jnp.dot(
                lhs_l[start : start + count], rhs_l[i], preferred_element_type=jnp.float32
            )
            if group == 0 and i:
                convert(i - 1)
            for first, row in tiles[len(tiles) * step // INNER : len(tiles) * (step + 1) // INNER]:
                table_tile(first, row)
            first = 0
            for (c, d), ref in zip(blocks, refs):
                mine = slice(first, first + block_rows(c))
                first += block_rows(c)
                sl = pl.ds(source(c, d), block_rows(c))
                new_real, new_imag = product[mine, :LANES], product[mine, LANES:]
                if step:
                    real, imag = acc[mine, :LANES], acc[mine, LANES:]
                    cos, sin = w[0, sl], w[1, sl]
                    new_real = real * cos + imag * sin + new_real
                    new_imag = imag * cos - real * sin + new_imag
                if i:
                    acc[mine, :LANES] = new_real
                    acc[mine, LANES:] = new_imag
                else:
                    cos, sin = pre[0, sl], pre[1, sl]
                    ref[:, :LANES] = (new_real * cos + new_imag * sin) * unscale
                    ref[:, LANES:] = (new_imag * cos - new_real * sin) * unscale

    sent = []

    def send(src, dst, sems, device):
        copy = pltpu.make_async_remote_copy(
            src_ref=src, dst_ref=dst, send_sem=sems[0], recv_sem=sems[1],
            device_id=device, device_id_type=MESH,
        )
        copy.start()
        sent.append(copy)
        return copy

    whole = slice(None)
    sent_by = {}
    last = {}

    def out_ref_of(c, d):
        if d == 0:
            return total[c]
        if CLASSES[c][0] == "b":
            return out[c].at[d % RING_Y - 1]
        return out[c].at[7 if d == 4 else abs(d) - 1 + (0 if d > 0 else 3)]

    def half_of(c, way):
        half = block_rows(c) // 2
        return pl.ds(half * way, half)

    def collect(c, way, far, ref):
        for d in (4, 3, 2, 1):
            if BEARER[d] == far:
                part = half_of(c, way) if d == 4 else whole
                sent_by[c, d, way].wait_recv()
                ref[part] += into[c][2 * (d - 1) + way, part]

    def leave(c, d):
        kind, count = CLASSES[c]
        if d == "own":
            if kind == "a":
                for way in range(2):
                    collect(c, way, 0, total[c])
                here, ring, device = y_here, RING_Y, at_y
            else:
                for slot in range(RING_Y - 1):
                    sent_by[c, slot].wait_recv()
                total[c][...] += into[c][0] + into[c][1] + into[c][2]
                here, ring, device = z_here, RING_Z, at_z
            last[c] = []
            for away in range(1, ring):
                start = pl.multiple_of((here + away) % ring * count, count)
                last[c].append(
                    send(
                        total[c].at[pl.ds(start, count)], second[c].at[away - 1],
                        (sems[c][2].at[away - 1], sems[c][3].at[away - 1]), device(away),
                    )
                )
        elif kind == "b":
            slot = d % RING_Y - 1
            sent_by[c, slot] = send(
                out[c].at[slot], into[c].at[slot], (sems[c][0].at[slot], sems[c][1].at[slot]), at_y(d)
            )
        else:
            far = abs(d)
            hops = far - BEARER[far]
            for way in (0, 1) if d == 4 else (int(d < 0),):
                part = half_of(c, way) if d == 4 else whole
                ref = out_ref_of(c, d)
                if far < 4:
                    collect(c, way, far, ref)
                slot = 2 * (far - 1) + way
                sent_by[c, far, way] = send(
                    ref.at[part], into[c].at[slot, part],
                    (sems[c][0].at[slot], sems[c][1].at[slot]), at_z(hops - 2 * hops * way),
                )

    for g, (blocks, messages) in enumerate(PLAN):
        work(g, [out_ref_of(c, d) for c, d in blocks])
        if g == 0:
            pl.semaphore_wait(barrier, len(partners))
        for c, d in messages:
            leave(c, d)

    pieces = []
    for c, (kind, count) in enumerate(CLASSES):
        place = y_here if kind == "a" else z_here
        piece = total[c][pl.ds(pl.multiple_of(place * count, count), count)]
        for d, copy in enumerate(last[c]):
            copy.wait_recv()
            piece = piece + second[c][d]
        pieces.append(piece)
    raw = jnp.concatenate(pieces, axis=0)

    real, imag = raw[:, :LANES], raw[:, LANES:]
    pad[:OWN] = real * real + imag * imag
    total = jnp.sum(pad[...].T, axis=0, keepdims=True)
    energy[...] = jnp.broadcast_to(total, energy.shape)
    copies = [
        send(energy, n_in.at[d - 1], (n_send.at[d - 1], n_recv.at[d - 1]), at_panel(d))
        for d in range(1, PANELS)
    ]
    for d, copy in enumerate(copies):
        copy.wait_recv()
        total = total + n_in[d, :1]
    scale = lax.rsqrt(total * (1.0 / (LANES * PANELS)) + 1e-06)
    scale = jnp.broadcast_to(scale, (LANES, LANES)).T[:OWN]
    out_ref[:, 0] = real * scale
    out_ref[:, 1] = imag * scale
    for copy in sent:
        copy.wait_send()


def fused(green_matrix, sign_bits, picks):
    f32, bf16 = jnp.float32, jnp.bfloat16
    wide = 2 * LANES
    return pl.pallas_call(
        kernel,
        out_shape=jax.ShapeDtypeStruct((OWN, 2, LANES), f32),
        in_specs=[
            pl.BlockSpec(memory_space=pl.ANY),
            pl.BlockSpec(memory_space=pltpu.VMEM),
            pl.BlockSpec(memory_space=pltpu.VMEM),
        ],
        out_specs=pl.BlockSpec(memory_space=pltpu.VMEM),
        scratch_shapes=[
            pltpu.VMEM((2, LOCAL, LANES), f32),
            pltpu.VMEM((2, 2, LOCAL // 2, LANES), f32),
            pltpu.VMEM((INNER, DEPTH, wide), bf16),
            pltpu.VMEM((INNER, 2 * DEPTH, wide), FINE),
            pltpu.VMEM((SKETCH, DEPTH), bf16),
            pltpu.VMEM((SKETCH, 2 * DEPTH), FINE),
            pltpu.VMEM((3, SKETCH, LANES), f32),
            pltpu.VMEM((2, SKETCH, LANES), f32),
            pltpu.VMEM((2, SKETCH, LANES), f32),
            pltpu.VMEM((LANES, LANES), f32),
            pltpu.VMEM((2, LANES, LANES), f32),
            pltpu.VMEM((MOST, wide), f32),
            pltpu.VMEM((8, LANES), f32),
            pltpu.VMEM((PANELS - 1, 8, LANES), f32),
            pltpu.SemaphoreType.DMA((8,)),
            pltpu.SemaphoreType.DMA((PANELS - 1,)),
            pltpu.SemaphoreType.DMA((PANELS - 1,)),
            [pltpu.VMEM((8 if kind == "a" else 3, block_rows(c), wide), f32) for c, (kind, _) in enumerate(CLASSES)],
            [pltpu.VMEM((8 if kind == "a" else 3, block_rows(c), wide), f32) for c, (kind, _) in enumerate(CLASSES)],
            [pltpu.VMEM((RING_Z - 1, count, wide), f32) for _, count in CLASSES],
            [pltpu.VMEM((block_rows(c), wide), f32) for c in range(len(CLASSES))],
            [[pltpu.SemaphoreType.DMA((8,))] * 4 for _ in CLASSES],
        ],
        compiler_params=pltpu.CompilerParams(
            collective_id=0, has_side_effects=True, vmem_limit_bytes=56 * 1024 * 1024
        ),
    )(green_matrix, sign_bits, picks)


def body(green_matrix, sign_bits, column_picks):
    return fused(green_matrix, sign_bits, column_picks)


def solution(mesh):
    placed = (P(None, "emit", "panel"), P("emit"), P())
    return jax.shard_map(
        body, mesh=mesh, in_specs=placed, out_specs=P("emit", None, "panel"), check_vma=False
    )
```
